32 devices in a mesh: seq: 8 (over z, x), head: 4 (over y, core).
Axes of the slice: x: 2, y: 2, z: 4, core: 2. Of those that a mesh axis runs over, the one named last changes fastest.
Arguments:
- queries: bfloat16 [8192, 32, 128], P('seq', 'head'), may hold values from -6 to 6
- seg_keys: bfloat16 [8192, 32, 128], P('seq', 'head'), may hold values from -6 to 6
- seg_values: bfloat16 [8192, 32, 128], P('seq', 'head'), may hold values from -6 to 6
- mem_keys: bfloat16 [32768, 32, 128], P('seq', 'head'), may hold values from -6 to 6
- mem_values: bfloat16 [32768, 32, 128], P('seq', 'head'), may hold values from -6 to 6
- mem_blocks: int32 [64, 4], P(('seq', 'head')), may hold values from 0 to 255, as said below
- mem_count: int32 [64], P(('seq', 'head')), may hold values from 1 to 4, as said below
- grad_out: bfloat16 [8192, 32, 128], P('seq', 'head'), may hold values from -6 to 6
Outputs:
- attn_out: bfloat16 [8192, 32, 128], P('seq', 'head')
- grad_q: bfloat16 [8192, 32, 128], P('seq', 'head')
- grad_k: bfloat16 [8192, 32, 128], P('seq', 'head')
- grad_v: bfloat16 [8192, 32, 128], P('seq', 'head')
The draws below stay inside these ranges and needn't reach their ends.
Inputs may be any that keep to these rules, and one draw needn't show every extreme that they name: `mem_blocks`: block n is held by owner n // 32. Among the 32 entries of the 8 query blocks of one seq shard (aligned blocks of 8 rows), at most 8 lie with one owner, and one owner has exactly 8 from every shard. Among the used entries (s < mem_count) of one seq shard at most 5 lie with one owner, and that same owner has exactly 5 used entries from every shard. `mem_count`: the counts of the 8 query blocks of one seq shard (aligned blocks of 8 rows) add up to 20, and in every such block of rows one count is 4.
All inputs are finite; a program needn't handle non-finite values.
Results may differ from the reference program's by a relative error of at most 0.012.
Values may be sent and summed in bfloat16 or wider, within the bound.
No kernel may reach another device: no remote copies, remote signals or barrier semaphores. Data moves between devices by JAX's collectives and lax.ppermute only.
A program may use at most 192 MiB of HBM per device.

```python
import math
import jax
import jax.numpy as jnp
from jax import lax

HEADS = 32
HEAD_DIM = 128
WINDOW = 1024
BLOCK = 128
TOPK = 4
MEM_DEV = 32
QB_DEV = 8
TOKENS = 8192
QBLOCKS = 64
OWNERS = 8
MEM_BLOCKS = 256
MEM_TOKENS = 32768
CAP = 8
LIVE_SUM = 20
LIVE_CAP = 5


def drawn_pair(key):
    shape = (TOKENS, HEADS, HEAD_DIM)
    query_draw = jnp.clip(jax.random.normal(jax.random.fold_in(key, 21), shape, jnp.float32), -6.0, 6.0)
    key_draw = jnp.clip(jax.random.normal(jax.random.fold_in(key, 22), shape, jnp.float32), -6.0, 6.0)
    return (query_draw, key_draw)


def draw_queries(key, part):
    return drawn_pair(key)[0].astype(jnp.bfloat16)


def draw_seg_keys(key, part):
    return drawn_pair(key)[1].astype(jnp.bfloat16)


def owner_series(hot_owner, per_owner, total, shuffle_key):
    others = (hot_owner + 1 + jnp.arange((OWNERS - 1) * per_owner, dtype=jnp.int32) // per_owner) % OWNERS
    others = jax.random.permutation(jax.random.fold_in(shuffle_key, 1), others)
    series = jnp.concatenate([jnp.full((per_owner,), hot_owner, jnp.int32), others])[:total]
    return jax.random.permutation(jax.random.fold_in(shuffle_key, 2), series)


def block_plan(key):
    slot_total = QB_DEV * TOPK
    units = QB_DEV * (TOPK - 1)
    extra = LIVE_SUM - QB_DEV
    dead_total = slot_total - LIVE_SUM
    hot_owner = jax.random.randint(jax.random.fold_in(key, 31), (), 0, OWNERS, dtype=jnp.int32)

    def one_shard(shard_id):
        shard_key = jax.random.fold_in(jax.random.fold_in(key, 32), shard_id)
        unit_block = jnp.arange(units, dtype=jnp.int32) // (TOPK - 1)
        full_block = jax.random.randint(jax.random.fold_in(shard_key, 4), (), 0, QB_DEV, dtype=jnp.int32)
        unit_rank = jax.random.permutation(jax.random.fold_in(shard_key, 5), units).astype(jnp.int32)
        unit_rank = jnp.where(unit_block == full_block, -1 - jnp.arange(units, dtype=jnp.int32) % (TOPK - 1), unit_rank)
        picked_order = jnp.argsort(unit_rank)
        chosen = jnp.zeros((units,), jnp.int32).at[picked_order[:extra]].set(1)
        counts = 1 + jnp.sum(chosen.reshape(QB_DEV, TOPK - 1), 1)
        live = (jnp.arange(TOPK, dtype=jnp.int32)[None, :] < counts[:, None]).reshape(-1)
        live_list = owner_series(hot_owner, LIVE_CAP, LIVE_SUM, jax.random.fold_in(shard_key, 6))
        dead_list = owner_series(hot_owner, CAP - LIVE_CAP, dead_total, jax.random.fold_in(shard_key, 7))
        place_rank = jnp.where(live, 0, slot_total) + jnp.arange(slot_total, dtype=jnp.int32)
        place_order = jnp.argsort(place_rank)
        owner_list = jnp.zeros((slot_total,), jnp.int32).at[place_order].set(jnp.concatenate([live_list, dead_list]))
        inside = jax.random.randint(jax.random.fold_in(shard_key, 3), (slot_total,), 0, MEM_DEV, dtype=jnp.int32)
        return ((owner_list * MEM_DEV + inside).reshape(QB_DEV, TOPK), counts.astype(jnp.int32))
    ids, counts = jax.vmap(one_shard)(jnp.arange(OWNERS, dtype=jnp.int32))
    return (ids.reshape(QBLOCKS, TOPK).astype(jnp.int32), counts.reshape(QBLOCKS).astype(jnp.int32))


def draw_mem_blocks(key, part):
    return block_plan(key)[0]


def draw_mem_count(key, part):
    return block_plan(key)[1]


def shard_levels(key, dims, split, least, high):
    gain = 1.0
    for axis_at, parts in split:
        draws = jax.random.uniform(jax.random.fold_in(jax.random.fold_in(key, 6), axis_at), (parts,), jnp.float32, least / len(split), high / len(split))
        gain = gain * jnp.repeat(jnp.exp(draws), dims[axis_at] // parts).reshape((-1,) + (1,) * (len(dims) - 1 - axis_at))
    return gain


def gaussian(key, dims, scale, reach, cuts=(), held_as=jnp.bfloat16):
    level = shard_levels(key, dims, cuts, -0.22, 0.18) if cuts else 1.0
    drawn = jax.random.normal(key, dims, jnp.float32) * scale * level
    return jnp.minimum(jnp.maximum(drawn, -reach), reach).astype(held_as)


def setup_inputs(seed: int = 0) -> dict:
    key_list = jax.random.split(jax.random.key(seed), 9)
    queries = draw_queries(jax.random.fold_in(key_list[8], 71), 0)
    seg_keys = draw_seg_keys(jax.random.fold_in(key_list[8], 71), 0)
    seg_values = gaussian(key_list[2], (TOKENS, HEADS, HEAD_DIM), 1.0, 6.0, ((0, 8), (1, 4)))
    mem_keys = gaussian(key_list[3], (MEM_TOKENS, HEADS, HEAD_DIM), 1.0, 6.0, ((0, 8), (1, 4)))
    mem_values = gaussian(key_list[4], (MEM_TOKENS, HEADS, HEAD_DIM), 1.0, 6.0, ((0, 8), (1, 4)))
    mem_blocks = draw_mem_blocks(jax.random.fold_in(key_list[8], 71), 0)
    mem_count = draw_mem_count(jax.random.fold_in(key_list[8], 71), 0)
    grad_out = gaussian(key_list[7], (TOKENS, HEADS, HEAD_DIM), 1.0, 6.0, ((0, 8), (1, 4)))
    return dict(queries=queries, seg_keys=seg_keys, seg_values=seg_values, mem_keys=mem_keys, mem_values=mem_values, mem_blocks=mem_blocks, mem_count=mem_count, grad_out=grad_out)


def settle(tensor):
    return lax.optimization_barrier(tensor.astype(jnp.bfloat16)).astype(jnp.float32)

def band_mask(query_pos, key_pos):
    gap_size = query_pos[:, None] - key_pos[None, :]
    return (gap_size >= 0) & (gap_size < WINDOW) & (key_pos[None, :] >= 0)

def reference(queries, seg_keys, seg_values, mem_keys, mem_values, mem_blocks, mem_count, grad_out):
    score_scale = 1.0 / math.sqrt(HEAD_DIM)
    span_keys = WINDOW + BLOCK
    mem_span = TOPK * BLOCK
    pad_rows = jnp.zeros((WINDOW, HEADS, HEAD_DIM), seg_keys.dtype)
    keys_padded = jnp.concatenate([pad_rows, seg_keys], 0)
    values_padded = jnp.concatenate([pad_rows, seg_values], 0)
    mem_key_blocks = mem_keys.reshape(MEM_BLOCKS, BLOCK, HEADS, HEAD_DIM)
    mem_value_blocks = mem_values.reshape(MEM_BLOCKS, BLOCK, HEADS, HEAD_DIM)

    def forward_block(block_id):
        row_start = block_id * BLOCK
        query_rows = lax.dynamic_slice_in_dim(queries, row_start, BLOCK, 0).astype(jnp.float32)
        grad_rows = lax.dynamic_slice_in_dim(grad_out, row_start, BLOCK, 0).astype(jnp.float32)
        key_window = lax.dynamic_slice_in_dim(keys_padded, row_start, span_keys, 0)
        value_window = lax.dynamic_slice_in_dim(values_padded, row_start, span_keys, 0)
        block_ids = lax.dynamic_index_in_dim(mem_blocks, block_id, 0, keepdims=False)
        used_count = lax.dynamic_index_in_dim(mem_count, block_id, 0, keepdims=False)
        mem_key_rows = jnp.take(mem_key_blocks, block_ids, axis=0).reshape(mem_span, HEADS, HEAD_DIM)
        mem_value_rows = jnp.take(mem_value_blocks, block_ids, axis=0).reshape(mem_span, HEADS, HEAD_DIM)
        combined_keys = jnp.concatenate([key_window, mem_key_rows], 0).astype(jnp.float32)
        combined_values = jnp.concatenate([value_window, mem_value_rows], 0).astype(jnp.float32)
        query_pos = row_start + jnp.arange(BLOCK, dtype=jnp.int32)
        key_pos = row_start - WINDOW + jnp.arange(span_keys, dtype=jnp.int32)
        mem_live = jnp.arange(mem_span, dtype=jnp.int32) // BLOCK < used_count
        key_live = jnp.concatenate([band_mask(query_pos, key_pos), jnp.broadcast_to(mem_live[None, :], (BLOCK, mem_span))], 1)
        scores = jnp.einsum('qhd,khd->hqk', query_rows, combined_keys) * score_scale
        scores = jnp.where(key_live[None], scores, -jnp.inf)
        row_top = lax.optimization_barrier(jnp.max(scores, -1, keepdims=True))
        log_total = row_top + jnp.log(lax.optimization_barrier(jnp.sum(jnp.exp(scores - row_top), -1, keepdims=True)))
        prob_full = jnp.exp(scores - log_total)
        attn_rows = jnp.einsum('hqk,khd->qhd', settle(prob_full), combined_values).astype(jnp.bfloat16)
        attn_back = lax.optimization_barrier(attn_rows).astype(jnp.float32)
        delta_rows = lax.optimization_barrier(jnp.sum(grad_rows * attn_back, -1))
        dprob = jnp.einsum('qhd,khd->hqk', grad_rows, combined_values)
        score_gradient = settle(prob_full * (dprob - delta_rows.T[:, :, None]))
        grad_rows_q = (score_scale * jnp.einsum('hqk,khd->qhd', score_gradient, combined_keys)).astype(jnp.bfloat16)
        return (attn_rows, grad_rows_q, log_total[:, :, 0].T, delta_rows)
    attn_blocks, gradq_blocks, lse_blocks, delta_blocks = lax.map(forward_block, jnp.arange(QBLOCKS, dtype=jnp.int32))
    attn_out = attn_blocks.reshape(TOKENS, HEADS, HEAD_DIM)
    grad_q = gradq_blocks.reshape(TOKENS, HEADS, HEAD_DIM)
    lse_all = lse_blocks.reshape(TOKENS, HEADS)
    delta_all = delta_blocks.reshape(TOKENS, HEADS)
    query_tail = jnp.zeros((WINDOW, HEADS, HEAD_DIM), queries.dtype)
    queries_padded = jnp.concatenate([queries, query_tail], 0)
    grads_padded = jnp.concatenate([grad_out, query_tail], 0)
    stat_tail = jnp.zeros((WINDOW, HEADS), jnp.float32)
    padded_log_sum_exp = jnp.concatenate([lse_all, stat_tail], 0)
    delta_padded = jnp.concatenate([delta_all, stat_tail], 0)

    def key_block(block_id):
        row_start = block_id * BLOCK
        key_rows = lax.dynamic_slice_in_dim(seg_keys, row_start, BLOCK, 0).astype(jnp.float32)
        value_rows = lax.dynamic_slice_in_dim(seg_values, row_start, BLOCK, 0).astype(jnp.float32)
        query_rows = lax.dynamic_slice_in_dim(queries_padded, row_start, span_keys, 0).astype(jnp.float32)
        grad_rows = lax.dynamic_slice_in_dim(grads_padded, row_start, span_keys, 0).astype(jnp.float32)
        lse_rows = lax.dynamic_slice_in_dim(padded_log_sum_exp, row_start, span_keys, 0)
        delta_rows = lax.dynamic_slice_in_dim(delta_padded, row_start, span_keys, 0)
        query_pos = row_start + jnp.arange(span_keys, dtype=jnp.int32)
        key_pos = row_start + jnp.arange(BLOCK, dtype=jnp.int32)
        key_live = band_mask(query_pos, key_pos) & (query_pos < TOKENS)[:, None]
        scores = jnp.einsum('qhd,khd->hqk', query_rows, key_rows) * score_scale
        prob_full = jnp.where(key_live[None], jnp.exp(scores - lse_rows.T[:, :, None]), 0.0)
        dprob = jnp.einsum('qhd,khd->hqk', grad_rows, value_rows)
        score_gradient = settle(prob_full * (dprob - delta_rows.T[:, :, None]))
        grad_rows_k = (score_scale * jnp.einsum('hqk,qhd->khd', score_gradient, query_rows)).astype(jnp.bfloat16)
        grad_rows_v = jnp.einsum('hqk,qhd->khd', settle(prob_full), grad_rows).astype(jnp.bfloat16)
        return (grad_rows_k, grad_rows_v)
    gradk_blocks, gradv_blocks = lax.map(key_block, jnp.arange(QBLOCKS, dtype=jnp.int32))
    grad_k = gradk_blocks.reshape(TOKENS, HEADS, HEAD_DIM)
    grad_v = gradv_blocks.reshape(TOKENS, HEADS, HEAD_DIM)
    return (attn_out, grad_q, grad_k, grad_v)
```

```python
import math

import jax
import jax.numpy as jnp
from jax import lax
from jax.experimental import pallas as pl
from jax.experimental.pallas import tpu as pltpu
from jax.sharding import PartitionSpec as P

WINDOW = 1024
BLOCK = 128
TOPK = 4
MASKED = -1e30
NT = (((1,), (1,)), ((), ()))
TN = (((0,), (0,)), ((), ()))
LOG2E = 1.4426950408889634


def dot(a, b, dims=(((1,), (0,)), ((), ()))):
    return lax.dot_general(a, b, dims, preferred_element_type=jnp.float32)


def attention_kernel(
    slot_ref, count_ref, first_ref, q_ref, g_ref, prev_ref, own_ref, mem_ref,
    o_ref, dq_ref, back_ref, dk_ref, dv_ref, kx, vx, dkx, dvx,
):
    tokens, head_dim = q_ref.shape
    span = WINDOW + BLOCK
    scale = 1.0 / math.sqrt(head_dim)
    kx[:WINDOW] = prev_ref[0]
    kx[WINDOW:] = own_ref[0]
    vx[:WINDOW] = prev_ref[1]
    vx[WINDOW:] = own_ref[1]
    dkx[...] = jnp.zeros_like(dkx)
    dvx[...] = jnp.zeros_like(dvx)
    start_col = first_ref[0] * WINDOW
    row = lax.broadcasted_iota(jnp.int32, (BLOCK, span), 0)
    col = lax.broadcasted_iota(jnp.int32, (BLOCK, span), 1)
    gap = col - row

    def block_step(b, carry):
        r0 = pl.multiple_of(b * BLOCK, BLOCK)
        rows = pl.ds(r0, BLOCK)
        window = pl.ds(r0, span)
        q = q_ref[rows, :]
        g = g_ref[rows, :]
        kw = kx[window, :]
        vw = vx[window, :]
        seen = (gap > 0) & (gap <= WINDOW) & (col >= start_col - r0)
        s = jnp.where(seen, dot(q, kw, NT) * (scale * LOG2E), MASKED)
        used = count_ref[b]
        km, vm, sm = [], [], []
        top = jnp.max(s, 1, keepdims=True)
        for i in range(TOPK):
            slot = slot_ref[b * TOPK + i]
            km.append(mem_ref[slot, 0])
            vm.append(mem_ref[slot, 1])
            far = dot(q, km[i], NT) * (scale * LOG2E)
            sm.append(jnp.where(i < used, far, MASKED))
            top = jnp.maximum(top, jnp.max(sm[i], 1, keepdims=True))
        p = jnp.exp2(s - top)
        total = jnp.sum(p, 1, keepdims=True)
        pm = []
        for i in range(TOPK):
            pm.append(jnp.exp2(sm[i] - top))
            total = total + jnp.sum(pm[i], 1, keepdims=True)
        inv = 1.0 / total
        p = p * inv
        pb = p.astype(jnp.bfloat16)
        o = dot(pb, vw)
        for i in range(TOPK):
            pm[i] = pm[i] * inv
            o = o + dot(pm[i].astype(jnp.bfloat16), vm[i])
        o = o.astype(jnp.bfloat16)
        o_ref[rows, :] = o
        delta = jnp.sum(g.astype(jnp.float32) * o.astype(jnp.float32), 1, keepdims=True)
        ds = (p * (dot(g, vw, NT) - delta)).astype(jnp.bfloat16)
        dq = dot(ds, kw)
        for i in range(TOPK):
            dsm = (pm[i] * (dot(g, vm[i], NT) - delta)).astype(jnp.bfloat16)
            dq = dq + dot(dsm, km[i])
        dq_ref[rows, :] = (dq * scale).astype(jnp.bfloat16)
        dkx[window, :] += dot(ds, q, TN)
        dvx[window, :] += dot(pb, g, TN)
        return carry

    lax.fori_loop(0, tokens // BLOCK, block_step, 0)
    back_ref[0] = (dkx[:WINDOW] * scale).astype(jnp.bfloat16)
    back_ref[1] = dvx[:WINDOW].astype(jnp.bfloat16)
    dk_ref[...] = dkx[WINDOW:] * scale
    dv_ref[...] = dvx[WINDOW:]


def attend(slots, counts, first, q, g, prev, own, mem):
    tokens, head_dim = q.shape
    ext = tokens + WINDOW
    vm = pl.BlockSpec(memory_space=pltpu.VMEM)
    sm = pl.BlockSpec(memory_space=pltpu.SMEM)
    row16 = jax.ShapeDtypeStruct((tokens, head_dim), jnp.bfloat16)
    row32 = jax.ShapeDtypeStruct((tokens, head_dim), jnp.float32)
    flops = 2 * tokens * head_dim * (6 * (WINDOW + BLOCK) + 4 * TOPK * BLOCK)
    return pl.pallas_call(
        attention_kernel,
        out_shape=(row16, row16, jax.ShapeDtypeStruct((2, WINDOW, head_dim), jnp.bfloat16), row32, row32),
        in_specs=[sm] * 3 + [vm] * 5,
        out_specs=[vm] * 5,
        scratch_shapes=[
            pltpu.VMEM((ext, head_dim), jnp.bfloat16),
            pltpu.VMEM((ext, head_dim), jnp.bfloat16),
            pltpu.VMEM((ext, head_dim), jnp.float32),
            pltpu.VMEM((ext, head_dim), jnp.float32),
        ],
        compiler_params=pltpu.CompilerParams(vmem_limit_bytes=32 << 20),
        cost_estimate=pl.CostEstimate(flops=flops, bytes_accessed=6 << 20, transcendentals=tokens * 1664),
        name="attend",
    )(slots, counts, first, q, g, prev, own, mem)


def shards(queries, seg_keys, seg_values, mem_keys, mem_values, mem_blocks, mem_count, grad_out):
    tokens, heads, head_dim = queries.shape
    owners = lax.axis_size("seq")
    rank = lax.axis_index("seq")
    n_blocks = tokens // BLOCK
    mem_local = mem_keys.shape[0] // BLOCK
    live_total = n_blocks * (TOPK + 1) // 2
    cap = max(2, 2 * live_total // owners)
    along = [(i, i + 1) for i in range(owners - 1)]
    back = [(i + 1, i) for i in range(owners - 1)]

    packed = jnp.concatenate([mem_blocks, mem_count[:, None]], 1)
    packed = lax.all_gather(packed, ("seq", "head"), axis=0, tiled=True)
    ids = packed[:, :TOPK].reshape(owners, n_blocks * TOPK)
    counts = packed[:, TOPK].reshape(owners, n_blocks)
    live = (jnp.arange(TOPK, dtype=jnp.int32)[None, None, :] < counts[:, :, None]).reshape(owners, -1)
    owner_of = ids // mem_local
    hot = (owner_of[:, :, None] == jnp.arange(owners, dtype=jnp.int32)) & live[:, :, None]
    order = jnp.sum((jnp.cumsum(hot.astype(jnp.int32), 1) - 1) * hot, 2)
    mine = (owner_of == rank) & live
    pick = mine[:, :, None] & (order[:, :, None] == jnp.arange(cap, dtype=jnp.int32))
    send_idx = jnp.sum(jnp.where(pick, (ids % mem_local)[:, :, None], 0), 1)
    send_idx = jnp.roll(send_idx, -rank, 0)
    slots = jnp.where(live, ((rank - owner_of) % owners) * cap + order, 0)
    slots = lax.dynamic_index_in_dim(slots, rank, 0, keepdims=False)
    my_counts = lax.dynamic_index_in_dim(counts, rank, 0, keepdims=False)
    first = (rank == 0).astype(jnp.int32)[None]

    q_major = jnp.moveaxis(queries, 1, 0)
    g_major = jnp.moveaxis(grad_out, 1, 0)
    kv_major = jnp.stack([jnp.moveaxis(seg_keys, 1, 0), jnp.moveaxis(seg_values, 1, 0)], 1)
    mem_major = jnp.stack(
        [
            jnp.moveaxis(m.reshape(mem_local, BLOCK, heads, head_dim), 2, 0)
            for m in (mem_keys, mem_values)
        ],
        2,
    )
    arrived, outs = [], []
    for h in range(heads):
        own = kv_major[h]
        send = mem_major[h][send_idx]
        if h >= 2:
            own, send, _ = lax.optimization_barrier((own, send, arrived[h - 2]))
        prev = lax.ppermute(own, "seq", along)
        parts = [send[0]] + [
            lax.ppermute(send[d], "seq", [(i, (i + d) % owners) for i in range(owners)])
            for d in range(1, owners)
        ]
        arrived.append((prev, parts))
    for h in range(heads):
        prev, parts = arrived[h]
        mem = jnp.concatenate(parts, 0)
        o, dq, ret, dk, dv = attend(slots, my_counts, first, q_major[h], g_major[h], prev, kv_major[h], mem)
        ret = lax.ppermute(ret, "seq", back).astype(jnp.float32)
        outs.append((o, dq, (dk + ret[0]).astype(jnp.bfloat16), (dv + ret[1]).astype(jnp.bfloat16)))
    return tuple(jnp.stack([o[i] for o in outs], 1) for i in range(4))


def solution(mesh):
    rows = P("seq", "head", None)
    return jax.shard_map(
        shards,
        mesh=mesh,
        in_specs=(rows, rows, rows, rows, rows, P(("seq", "head"), None), P(("seq", "head")), rows),
        out_specs=(rows, rows, rows, rows),
        check_vma=False,
    )
```

```python
import functools
import math

import jax
import jax.numpy as jnp
from jax import lax
from jax.experimental import pallas as pl
from jax.experimental.pallas import tpu as pltpu
from jax.sharding import PartitionSpec as P

WINDOW = 1024
BLOCK = 128
TOPK = 4
COLUMNS = 2
ROWS = 4
MASKED = -1e30
LAG = 2
FAR = 256
NT = (((1,), (1,)), ((), ()))
TN = (((0,), (0,)), ((), ()))
LOG2E = 1.4426950408889634
VM = pl.BlockSpec(memory_space=pltpu.VMEM)
SM = pl.BlockSpec(memory_space=pltpu.SMEM)
ANY = pl.BlockSpec(memory_space=pl.ANY)


def dot(a, b, dims=(((1,), (0,)), ((), ()))):
    return lax.dot_general(a, b, dims, preferred_element_type=jnp.float32)


def route_kernel(cap, per, list_ref, rank_ref, pick_ref, pack_ref, final_ref, count_ref, need_ref, seen, lines):
    owners = ROWS * COLUMNS
    row_len = TOPK + 1
    blocks = list_ref.shape[1] // row_len
    me = rank_ref[0]
    my_row, my_col = me // COLUMNS, me % COLUMNS
    for ref in (pick_ref, pack_ref, final_ref):
        for i in range(ref.shape[0]):
            ref[i] = 0
    need_ref[0] = 0

    def reader_block(step, carry):
        reader, block = lax.div(step, blocks), lax.rem(step, blocks)
        to_row, to_col = lax.div(reader, COLUMNS), lax.rem(reader, COLUMNS)
        place = reader ^ me

        @pl.when(block == 0)
        def _():
            for o in range(owners):
                seen[o] = 0
            for r in range(ROWS):
                lines[r] = 0

        used = list_ref[place, block * row_len + TOPK]

        @pl.when(reader == me)
        def _():
            count_ref[block] = used

        for s in range(TOPK):

            @pl.when(s < used)
            def _():
                entry = list_ref[place, block * row_len + s]
                owner = lax.div(entry, per)
                inside = entry - owner * per
                order = seen[owner]
                seen[owner] = order + 1
                row, col = lax.div(owner, COLUMNS), lax.rem(owner, COLUMNS)
                moved = (col != to_col).astype(jnp.int32)
                distance = row ^ to_row
                spot = lines[row]
                lines[row] = spot + 1

                @pl.when(distance > 0)
                def _():
                    need_ref[0] = jnp.maximum(need_ref[0], spot + 1)

                @pl.when(owner == me)
                def _():
                    pick_ref[(moved * ROWS + distance) * cap + order] = inside

                @pl.when((distance > 0) & (row == my_row) & (to_col == my_col))
                def _():
                    pack_ref[(distance - 1) * 2 * cap + spot] = (moved * (ROWS - 1) + distance - 1) * cap + order

                @pl.when(reader == me)
                def _():
                    final_ref[block * TOPK + s] = jnp.where(distance == 0, moved * cap + order, distance * FAR + spot)

        return carry

    lax.fori_loop(0, owners * blocks, reader_block, 0)


def route(lists, rank, cap, per):
    owners, width = lists.shape
    blocks = width // (TOPK + 1)
    i32 = lambda n: jax.ShapeDtypeStruct((n,), jnp.int32)
    return pl.pallas_call(
        functools.partial(route_kernel, cap, per),
        out_shape=(i32(2 * ROWS * cap), i32(2 * (ROWS - 1) * cap), i32(blocks * TOPK), i32(blocks), i32(1)),
        in_specs=[SM, SM],
        out_specs=[SM] * 5,
        scratch_shapes=[pltpu.SMEM((owners,), jnp.int32), pltpu.SMEM((ROWS,), jnp.int32)],
        name="route",
    )(lists, rank)


def pick_kernel(table_ref, key_ref, value_ref, *outs):
    first = 0
    for out in outs:

        def place(i, carry, out=out, first=first):
            at = table_ref[first + i]
            out[i, 0] = key_ref[at]
            out[i, 1] = value_ref[at]
            return carry

        lax.fori_loop(0, out.shape[0], place, 0)
        first += out.shape[0]


def pick(head, table, keys, values):
    head_dim = keys.shape[-1]
    whole = pl.BlockSpec((None,) + keys.shape[1:], lambda i: (head, 0, 0, 0))
    size = table.shape[0] // 2
    return pl.pallas_call(
        pick_kernel,
        grid=(1,),
        out_shape=[jax.ShapeDtypeStruct((size, 2, BLOCK, head_dim), keys.dtype)] * 2,
        in_specs=[SM, whole, whole],
        out_specs=[pl.BlockSpec((size, 2, BLOCK, head_dim), lambda i: (0, 0, 0, 0))] * 2,
        compiler_params=pltpu.CompilerParams(vmem_limit_bytes=32 << 20),
        cost_estimate=pl.CostEstimate(flops=0, bytes_accessed=1 << 16, transcendentals=0),
        name="pick",
    )(table, keys, values)


def pack_kernel(cap, table_ref, stay_ref, side_ref, *rest):
    *outs, held, sem = rest
    size = (ROWS - 1) * cap
    moves = [
        pltpu.make_async_copy(ref.at[cap:], held.at[i * size : (i + 1) * size], sem.at[i])
        for i, ref in enumerate((stay_ref, side_ref))
    ]
    for move in moves:
        move.start()
    for move in moves:
        move.wait()
    for d, out in enumerate(outs):

        def place(i, carry, d=d, out=out):
            out[i] = held[table_ref[d * 2 * cap + i]]
            return carry

        lax.fori_loop(0, out.shape[0], place, 0)


def pack(cap, length, table, stay, side):
    block = stay.shape[1:]
    return pl.pallas_call(
        functools.partial(pack_kernel, cap),
        out_shape=[jax.ShapeDtypeStruct((length,) + block, stay.dtype)] * (ROWS - 1),
        in_specs=[SM, ANY, ANY],
        out_specs=[VM] * (ROWS - 1),
        scratch_shapes=[
            pltpu.VMEM((2 * (ROWS - 1) * cap,) + block, stay.dtype), pltpu.SemaphoreType.DMA((2,))
        ],
        compiler_params=pltpu.CompilerParams(vmem_limit_bytes=16 << 20),
        cost_estimate=pl.CostEstimate(flops=0, bytes_accessed=1 << 16, transcendentals=0),
        name="pack",
    )(table, stay, side)


def attention_kernel(
    cap, final_ref, count_ref, first_ref, qg_ref, prev_ref, own_ref, *rest
):
    *sources, o_ref, dq_ref, stat_ref, dk_ref, dv_ref, mem, kx, vx, dkx, dvx, sem = rest
    tokens, head_dim = qg_ref.shape[1:]
    span = WINDOW + BLOCK
    scale = 1.0 / math.sqrt(head_dim)
    moves, at = [], 0
    for i, ref in enumerate(sources):
        size = cap if i < 2 else ref.shape[0]
        moves.append(pltpu.make_async_copy(ref.at[:size], mem.at[at : at + size], sem.at[i]))
        moves[i].start()
        at += size
    far_size = sources[-1].shape[0]
    kx[:WINDOW] = prev_ref[0]
    kx[WINDOW:] = own_ref[0]
    vx[:WINDOW] = prev_ref[1]
    vx[WINDOW:] = own_ref[1]
    dkx[...] = jnp.zeros_like(dkx)
    dvx[...] = jnp.zeros_like(dvx)
    for move in moves:
        move.wait()
    start_col = first_ref[0] * WINDOW
    row = lax.broadcasted_iota(jnp.int32, (BLOCK, span), 0)
    col = lax.broadcasted_iota(jnp.int32, (BLOCK, span), 1)
    gap = col - row
    lane = lax.broadcasted_iota(jnp.int32, (BLOCK, BLOCK), 1)

    def block_step(b, carry):
        r0 = pl.multiple_of(b * BLOCK, BLOCK)
        rows = pl.ds(r0, BLOCK)
        window = pl.ds(r0, span)
        q = qg_ref[0, rows, :]
        g = qg_ref[1, rows, :]
        kw = kx[window, :]
        vw = vx[window, :]
        seen = (gap > 0) & (gap <= WINDOW) & (col >= start_col - r0)
        s = jnp.where(seen, dot(q, kw, NT) * (scale * LOG2E), MASKED)
        used = count_ref[b]
        km, vm, sm = [], [], []
        top = jnp.max(s, 1, keepdims=True)
        for i in range(TOPK):
            code = final_ref[b * TOPK + i]
            line, slot = code // FAR, code % FAR
            slot = jnp.where(line == 0, slot, 2 * cap + (line - 1) * far_size + slot)
            km.append(mem[slot, 0])
            vm.append(mem[slot, 1])
            far = dot(q, km[i], NT) * (scale * LOG2E)
            sm.append(jnp.where(i < used, far, MASKED))
            top = jnp.maximum(top, jnp.max(sm[i], 1, keepdims=True))
        p = jnp.exp2(s - top)
        total = jnp.sum(p, 1, keepdims=True)
        pm = []
        for i in range(TOPK):
            pm.append(jnp.exp2(sm[i] - top))
            total = total + jnp.sum(pm[i], 1, keepdims=True)
        inv = 1.0 / total
        p = p * inv
        pb = p.astype(jnp.bfloat16)
        o = dot(pb, vw)
        for i in range(TOPK):
            pm[i] = pm[i] * inv
            o = o + dot(pm[i].astype(jnp.bfloat16), vm[i])
        o = o.astype(jnp.bfloat16)
        o_ref[rows, :] = o
        delta = jnp.sum(g.astype(jnp.float32) * o.astype(jnp.float32), 1, keepdims=True)
        ds = (p * (dot(g, vw, NT) - delta)).astype(jnp.bfloat16)
        dq = dot(ds, kw)
        for i in range(TOPK):
            dsm = (pm[i] * (dot(g, vm[i], NT) - delta)).astype(jnp.bfloat16)
            dq = dq + dot(dsm, km[i])
        dq_ref[rows, :] = (dq * scale).astype(jnp.bfloat16)
        both = jnp.where(lane < BLOCK // 2, top + jnp.log2(total), delta).T
        stat_ref[0:1, rows] = both[0:1]
        stat_ref[1:2, rows] = both[BLOCK // 2 : BLOCK // 2 + 1]
        dkx[window, :] += dot(ds, q, TN)
        dvx[window, :] += dot(pb, g, TN)
        return carry

    lax.fori_loop(0, tokens // BLOCK, block_step, 0)
    dk_ref[...] = dkx[WINDOW:]
    dv_ref[...] = dvx[WINDOW:]


def of_head(head, a):
    return pl.BlockSpec((a.shape[0], None) + a.shape[2:], lambda i: (0, head, 0, 0))


def attend(cap, final, counts, first, head, qg, at, prev, own, *sources):
    tokens, head_dim = qg.shape[2:]
    ext = tokens + WINDOW
    slots = 2 * cap + sum(s.shape[0] for s in sources[2:])
    row16 = jax.ShapeDtypeStruct((tokens, head_dim), jnp.bfloat16)
    row32 = jax.ShapeDtypeStruct((tokens, head_dim), jnp.float32)
    return pl.pallas_call(
        functools.partial(attention_kernel, cap),
        out_shape=(row16, row16, jax.ShapeDtypeStruct((2, tokens), jnp.float32), row32, row32),
        grid=(1,),
        in_specs=[SM] * 3 + [of_head(head, qg), of_head(at, prev), of_head(head, own)] + [ANY] * len(sources),
        out_specs=[VM] * 5,
        scratch_shapes=[
            pltpu.VMEM((slots, 2, BLOCK, head_dim), jnp.bfloat16),
            pltpu.VMEM((ext, head_dim), jnp.bfloat16),
            pltpu.VMEM((ext, head_dim), jnp.bfloat16),
            pltpu.VMEM((ext, head_dim), jnp.float32),
            pltpu.VMEM((ext, head_dim), jnp.float32),
            pltpu.SemaphoreType.DMA((len(sources),)),
        ],
        compiler_params=pltpu.CompilerParams(vmem_limit_bytes=32 << 20),
        cost_estimate=pl.CostEstimate(flops=128 * tokens * tokens * head_dim, bytes_accessed=1 << 16, transcendentals=0),
        name="attend",
    )(final, counts, first, qg, prev, own, *sources)


def back_kernel(stat_ref, next_ref, own_ref, dk_in, dv_in, dk_ref, dv_ref):
    tokens, head_dim = dk_in.shape
    scale = 1.0 / math.sqrt(head_dim)
    size = 2 * BLOCK
    for j in range(tokens // size):
        rows = slice(j * size, (j + 1) * size)
        seen = (j + 1) * size
        k, v = own_ref[0, rows], own_ref[1, rows]
        q, g = next_ref[0, :seen], next_ref[1, :seen]
        key = lax.broadcasted_iota(jnp.int32, (size, seen), 0) + j * size
        query = lax.broadcasted_iota(jnp.int32, (size, seen), 1)
        s = dot(k, q, NT) * (scale * LOG2E) - stat_ref[0:1, :seen]
        p = jnp.exp2(jnp.where(key > query, s, MASKED))
        ds = (p * (dot(v, g, NT) - stat_ref[1:2, :seen])).astype(jnp.bfloat16)
        dk_ref[rows] = ((dk_in[rows] + dot(ds, q)) * scale).astype(jnp.bfloat16)
        dv_ref[rows] = (dv_in[rows] + dot(p.astype(jnp.bfloat16), g)).astype(jnp.bfloat16)


def add_back(head, stat, at, following, own, dk, dv):
    tokens, head_dim = dk.shape
    row16 = jax.ShapeDtypeStruct((tokens, head_dim), jnp.bfloat16)
    return pl.pallas_call(
        back_kernel,
        out_shape=(row16, row16),
        grid=(1,),
        in_specs=[VM, of_head(at, following), of_head(head, own), VM, VM],
        out_specs=[VM] * 2,
        compiler_params=pltpu.CompilerParams(vmem_limit_bytes=32 << 20),
        cost_estimate=pl.CostEstimate(flops=0, bytes_accessed=1 << 16, transcendentals=0),
        name="add_back",
    )(stat, following, own, dk, dv)


def after(x, *earlier):
    earlier = [e for e in earlier if e is not None]
    return lax.optimization_barrier((x, *earlier))[0] if earlier else x


def shards(queries, seg_keys, seg_values, mem_keys, mem_values, mem_blocks, mem_count, grad_out):
    tokens, heads, head_dim = queries.shape
    owners = lax.axis_size("seq")
    rank = lax.axis_index("seq")
    n_blocks = tokens // BLOCK
    per = mem_keys.shape[0] // BLOCK
    live_total = n_blocks * (TOPK + 1) // 2
    cap = max(2, 2 * live_total // owners)
    along = [(i, i + 1) for i in range(owners - 1)]
    back = [(i + 1, i) for i in range(owners - 1)]
    shift = lambda d: [(i, (i + d) % owners) for i in range(owners)]

    lists = jnp.concatenate([mem_blocks, mem_count[:, None]], 1)
    lists = lax.all_gather(lists, "head", axis=0, tiled=True).reshape(1, -1)
    while lists.shape[0] < owners:
        size = lists.shape[0]
        with jax.named_scope(f"lists{size}"):
            theirs = lax.ppermute(lists, "seq", [(i, i ^ size) for i in range(owners)])
        lists = jnp.concatenate([lists, theirs], 0)

    first = (rank == 0).astype(jnp.int32)[None]
    major = lambda a: jnp.moveaxis(a, 1, 0)
    kv = jnp.stack([major(seg_keys), major(seg_values)], 0)
    qg = jnp.stack([major(queries), major(grad_out)], 0)

    held_keys, held_values = after((mem_keys, mem_values), lists)
    keys, values = (
        jnp.moveaxis(m.reshape(per, BLOCK, heads, head_dim), 2, 0) for m in (held_keys, held_values)
    )

    def border(cut, *earlier):
        up, down = after((kv[:, cut], qg[:, cut]), *earlier)
        with jax.named_scope(f"prev_kv{cut.start}"):
            up = lax.ppermute(up, "seq", along)
        with jax.named_scope(f"next_qg{cut.start}"):
            down = lax.ppermute(down, "seq", back)
        return up, down

    def in_rows(outs):
        return tuple(jnp.stack([o[i] for o in outs], 1) for i in range(4))

    def finish(head, final, counts, borders, *sources):
        prev_kv, next_qg, at = borders[head]
        o, dq, stat, dk, dv = attend(
            cap, final, counts, first, head, qg, at, prev_kv, kv, *sources
        )
        with jax.named_scope(f"stat{head}"):
            stat = lax.ppermute(stat, "seq", back)
        dk, dv = add_back(head, stat, at, next_qg, kv, dk, dv)
        return o, dq, dk, dv

    def direct():
        packed = lists[jnp.arange(owners) ^ rank].reshape(owners, n_blocks, TOPK + 1)
        ids = packed[:, :, :TOPK].reshape(owners, n_blocks * TOPK)
        counts = packed[:, :, TOPK]
        live = (jnp.arange(TOPK, dtype=jnp.int32) < counts[:, :, None]).reshape(owners, -1)
        owner_of = ids // per
        one_hot = (owner_of[:, :, None] == jnp.arange(owners, dtype=jnp.int32)) & live[:, :, None]
        order = jnp.sum((jnp.cumsum(one_hot.astype(jnp.int32), 1) - 1) * one_hot, 2)
        asked = (owner_of == rank) & live
        chosen = asked[:, :, None] & (order[:, :, None] == jnp.arange(cap, dtype=jnp.int32))
        send_idx = jnp.roll(jnp.sum(jnp.where(chosen, (ids % per)[:, :, None], 0), 1), -rank, 0)
        final = jnp.where(live, ((rank - owner_of) % owners) * cap + order, 0)
        final = lax.dynamic_index_in_dim(final, rank, 0, keepdims=False)
        counts = lax.dynamic_index_in_dim(counts, rank, 0, keepdims=False)
        borders = [border(slice(h, h + 1)) + (0,) for h in range(heads)]
        arrived = []
        for h in range(heads):
            send = jnp.stack([keys[h][send_idx], values[h][send_idx]], 2)
            if h >= 2:
                send = after(send, *arrived[h - 2])
            arrived.append([send[0]] + [lax.ppermute(send[d], "seq", shift(d)) for d in range(1, owners)])
        return in_rows([finish(h, final, counts, borders, *arrived[h]) for h in range(heads)])

    if owners != ROWS * COLUMNS:
        return direct()

    pick_table, pack_table, final, counts, need = route(lists, rank[None], cap, per)
    early = min(2, heads)
    first_border = border(slice(0, early), lists)

    def by_rows(length):
        picked = [pick(h, pick_table, keys, values) for h in range(heads)]
        swap = [(i, i ^ 1) for i in range(owners)]
        with jax.named_scope("side0"):
            side = [lax.ppermute(picked[0][1], "seq", swap)]
        borders = [first_border + (h,) for h in range(early)]
        lines, outs = [], []

        def complete(h):
            ready = after(counts, lines[h + 1][2]) if h + 1 < heads else counts
            outs.append(finish(h, final, ready, borders, picked[h][0], side[h], *lines[h]))

        earlier = list(first_border)
        for h in range(heads):
            sends = list(pack(cap, length, pack_table, picked[h][0], side[h]))
            if h + 1 < heads:
                sends.append(picked[h + 1][1])
            if h + early < heads:
                cut = slice(h + early, h + early + 1)
                sends += [kv[:, cut], qg[:, cut]]
            sends = list(lax.optimization_barrier((sends, earlier))[0])
            sent = []
            for d in range(ROWS - 1):
                with jax.named_scope(f"lines{h}_{d}"):
                    route = [(i, i ^ (COLUMNS * (d + 1))) for i in range(owners)]
                    sent.append(lax.ppermute(sends[d], "seq", route))
            lines.append(sent)
            earlier = list(sent)
            if h + 1 < heads:
                with jax.named_scope(f"side{h + 1}"):
                    side.append(lax.ppermute(sends[3], "seq", swap))
                earlier.append(side[h + 1])
            if h + early < heads:
                with jax.named_scope(f"prev_kv{h + early}"):
                    up = lax.ppermute(sends[4], "seq", along)
                with jax.named_scope(f"next_qg{h + early}"):
                    down = lax.ppermute(sends[5], "seq", back)
                borders.append((up, down, 0))
                earlier += [up, down]
            if h >= 1:
                complete(h - 1)
                earlier.append(outs[h - 1][0])
            if h >= 2:
                earlier.append(outs[h - 2][2])
        complete(heads - 1)
        return in_rows(outs)

    longest = 2 * cap
    sizes = [longest - 2, longest - 1, longest]
    index = jnp.clip(need[0] - sizes[0], 0, 2)
    return lax.switch(index, [functools.partial(by_rows, n) for n in sizes])


def solution(mesh):
    rows = P("seq", "head", None)
    return jax.shard_map(
        shards,
        mesh=mesh,
        in_specs=(rows, rows, rows, rows, rows, P(("seq", "head"), None), P(("seq", "head")), rows),
        out_specs=(rows, rows, rows, rows),
        check_vma=False,
    )
```

```python
import functools
import math

import jax
import jax.numpy as jnp
from jax import lax
from jax.experimental import pallas as pl
from jax.experimental.pallas import tpu as pltpu
from jax.sharding import PartitionSpec as P

WINDOW = 1024
BLOCK = 128
TOPK = 4
COLUMNS = 2
ROWS = 4
MASKED = -1e30
LAG = 2
FAR = 256
NT = (((1,), (1,)), ((), ()))
TN = (((0,), (0,)), ((), ()))
LOG2E = 1.4426950408889634
VM = pl.BlockSpec(memory_space=pltpu.VMEM)
SM = pl.BlockSpec(memory_space=pltpu.SMEM)
ANY = pl.BlockSpec(memory_space=pl.ANY)


def dot(a, b, dims=(((1,), (0,)), ((), ()))):
    return lax.dot_general(a, b, dims, preferred_element_type=jnp.float32)


def route_kernel(cap, per, list_ref, rank_ref, pick_ref, pack_ref, final_ref, count_ref, need_ref, seen, lines):
    owners = ROWS * COLUMNS
    row_len = TOPK + 1
    blocks = list_ref.shape[1] // row_len
    me = rank_ref[0]
    my_row, my_col = me // COLUMNS, me % COLUMNS
    for ref in (pick_ref, pack_ref, final_ref):
        for i in range(ref.shape[0]):
            ref[i] = 0
    need_ref[0] = 0

    def reader_block(step, carry):
        reader, block = lax.div(step, blocks), lax.rem(step, blocks)
        to_row, to_col = lax.div(reader, COLUMNS), lax.rem(reader, COLUMNS)
        place = reader ^ me

        @pl.when(block == 0)
        def _():
            for o in range(owners):
                seen[o] = 0
            for r in range(ROWS):
                lines[r] = 0

        used = list_ref[place, block * row_len + TOPK]

        @pl.when(reader == me)
        def _():
            count_ref[block] = used

        for s in range(TOPK):

            @pl.when(s < used)
            def _():
                entry = list_ref[place, block * row_len + s]
                owner = lax.div(entry, per)
                inside = entry - owner * per
                order = seen[owner]
                seen[owner] = order + 1
                row, col = lax.div(owner, COLUMNS), lax.rem(owner, COLUMNS)
                moved = (col != to_col).astype(jnp.int32)
                distance = row ^ to_row
                spot = lines[row]
                lines[row] = spot + 1

                @pl.when(distance > 1)
                def _():
                    need_ref[0] = jnp.maximum(need_ref[0], spot + 1)

                @pl.when(owner == me)
                def _():
                    pick_ref[(moved * ROWS + distance) * cap + order] = inside

                @pl.when((distance > 0) & (row == my_row) & (to_col == my_col))
                def _():
                    pack_ref[(distance - 1) * 2 * cap + spot] = (moved * (ROWS - 1) + distance - 1) * cap + order

                @pl.when(reader == me)
                def _():
                    final_ref[block * TOPK + s] = jnp.where(distance == 0, moved * cap + order, distance * FAR + spot)

        return carry

    lax.fori_loop(0, owners * blocks, reader_block, 0)


def route(lists, rank, cap, per):
    owners, width = lists.shape
    blocks = width // (TOPK + 1)
    i32 = lambda n: jax.ShapeDtypeStruct((n,), jnp.int32)
    return pl.pallas_call(
        functools.partial(route_kernel, cap, per),
        out_shape=(i32(2 * ROWS * cap), i32(2 * (ROWS - 1) * cap), i32(blocks * TOPK), i32(blocks), i32(1)),
        in_specs=[SM, SM],
        out_specs=[SM] * 5,
        scratch_shapes=[pltpu.SMEM((owners,), jnp.int32), pltpu.SMEM((ROWS,), jnp.int32)],
        name="route",
    )(lists, rank)


def pick_kernel(table_ref, key_ref, value_ref, *outs):
    first = 0
    for out in outs:

        def place(i, carry, out=out, first=first):
            at = table_ref[first + i]
            out[i, 0] = key_ref[at]
            out[i, 1] = value_ref[at]
            return carry

        lax.fori_loop(0, out.shape[0], place, 0)
        first += out.shape[0]


def pick(head, table, keys, values):
    head_dim = keys.shape[-1]
    whole = pl.BlockSpec((None,) + keys.shape[1:], lambda i: (head, 0, 0, 0))
    size = table.shape[0] // 2
    return pl.pallas_call(
        pick_kernel,
        grid=(1,),
        out_shape=[jax.ShapeDtypeStruct((size, 2, BLOCK, head_dim), keys.dtype)] * 2,
        in_specs=[SM, whole, whole],
        out_specs=[pl.BlockSpec((size, 2, BLOCK, head_dim), lambda i: (0, 0, 0, 0))] * 2,
        compiler_params=pltpu.CompilerParams(vmem_limit_bytes=32 << 20),
        cost_estimate=pl.CostEstimate(flops=0, bytes_accessed=1 << 16, transcendentals=0),
        name="pick",
    )(table, keys, values)


def pack_kernel(cap, table_ref, stay_ref, side_ref, *rest):
    *outs, held, sem = rest
    size = (ROWS - 1) * cap
    moves = [
        pltpu.make_async_copy(ref.at[cap : ROWS * cap], held.at[i * size : (i + 1) * size], sem.at[i])
        for i, ref in enumerate((stay_ref, side_ref))
    ]
    for move in moves:
        move.start()
    for move in moves:
        move.wait()
    for d, out in enumerate(outs):

        def place(i, carry, d=d, out=out):
            out[i] = held[table_ref[d * 2 * cap + i]]
            return carry

        lax.fori_loop(0, out.shape[0], place, 0)


def pack(cap, lengths, table, stay, side):
    block = stay.shape[1:]
    return pl.pallas_call(
        functools.partial(pack_kernel, cap),
        out_shape=[jax.ShapeDtypeStruct((n,) + block, stay.dtype) for n in lengths],
        in_specs=[SM, ANY, ANY],
        out_specs=[VM] * (ROWS - 1),
        scratch_shapes=[
            pltpu.VMEM((2 * (ROWS - 1) * cap,) + block, stay.dtype), pltpu.SemaphoreType.DMA((2,))
        ],
        compiler_params=pltpu.CompilerParams(vmem_limit_bytes=16 << 20),
        cost_estimate=pl.CostEstimate(flops=0, bytes_accessed=1 << 16, transcendentals=0),
        name="pack",
    )(table, stay, side)


def attention_kernel(
    cap, final_ref, count_ref, first_ref, qg_ref, prev_ref, own_ref, *rest
):
    *sources, o_ref, dq_ref, stat_ref, dk_ref, dv_ref, mem, kx, vx, dkx, dvx, sem = rest
    tokens, head_dim = qg_ref.shape[1:]
    span = WINDOW + BLOCK
    scale = 1.0 / math.sqrt(head_dim)
    moves, at = [], 0
    for i, ref in enumerate(sources):
        size = cap if i < 2 else ref.shape[0]
        moves.append(pltpu.make_async_copy(ref.at[:size], mem.at[at : at + size], sem.at[i]))
        moves[i].start()
        at += size
    near_size, far_size = sources[2].shape[0], sources[-1].shape[0]
    kx[:WINDOW] = prev_ref[0]
    kx[WINDOW:] = own_ref[0]
    vx[:WINDOW] = prev_ref[1]
    vx[WINDOW:] = own_ref[1]
    dkx[...] = jnp.zeros_like(dkx)
    dvx[...] = jnp.zeros_like(dvx)
    for move in moves:
        move.wait()
    start_col = first_ref[0] * WINDOW
    row = lax.broadcasted_iota(jnp.int32, (BLOCK, span), 0)
    col = lax.broadcasted_iota(jnp.int32, (BLOCK, span), 1)
    gap = col - row
    lane = lax.broadcasted_iota(jnp.int32, (BLOCK, BLOCK), 1)

    def block_step(b, carry):
        r0 = pl.multiple_of(b * BLOCK, BLOCK)
        rows = pl.ds(r0, BLOCK)
        window = pl.ds(r0, span)
        q = qg_ref[0, rows, :]
        g = qg_ref[1, rows, :]
        kw = kx[window, :]
        vw = vx[window, :]
        seen = (gap > 0) & (gap <= WINDOW) & (col >= start_col - r0)
        s = jnp.where(seen, dot(q, kw, NT) * (scale * LOG2E), MASKED)
        used = count_ref[b]
        km, vm, sm = [], [], []
        top = jnp.max(s, 1, keepdims=True)
        for i in range(TOPK):
            code = final_ref[b * TOPK + i]
            line, slot = code // FAR, code % FAR
            away = 2 * cap + jnp.where(line > 1, near_size + (line - 2) * far_size, 0)
            slot = jnp.where(line == 0, slot, away + slot)
            km.append(mem[slot, 0])
            vm.append(mem[slot, 1])
            far = dot(q, km[i], NT) * (scale * LOG2E)
            sm.append(jnp.where(i < used, far, MASKED))
            top = jnp.maximum(top, jnp.max(sm[i], 1, keepdims=True))
        p = jnp.exp2(s - top)
        total = jnp.sum(p, 1, keepdims=True)
        pm = []
        for i in range(TOPK):
            pm.append(jnp.exp2(sm[i] - top))
            total = total + jnp.sum(pm[i], 1, keepdims=True)
        inv = 1.0 / total
        p = p * inv
        pb = p.astype(jnp.bfloat16)
        o = dot(pb, vw)
        for i in range(TOPK):
            pm[i] = pm[i] * inv
            o = o + dot(pm[i].astype(jnp.bfloat16), vm[i])
        o = o.astype(jnp.bfloat16)
        o_ref[rows, :] = o
        delta = jnp.sum(g.astype(jnp.float32) * o.astype(jnp.float32), 1, keepdims=True)
        ds = (p * (dot(g, vw, NT) - delta)).astype(jnp.bfloat16)
        dq = dot(ds, kw)
        for i in range(TOPK):
            dsm = (pm[i] * (dot(g, vm[i], NT) - delta)).astype(jnp.bfloat16)
            dq = dq + dot(dsm, km[i])
        dq_ref[rows, :] = (dq * scale).astype(jnp.bfloat16)
        both = jnp.where(lane < BLOCK // 2, top + jnp.log2(total), delta).T
        stat_ref[0:1, rows] = both[0:1]
        stat_ref[1:2, rows] = both[BLOCK // 2 : BLOCK // 2 + 1]
        dkx[window, :] += dot(ds, q, TN)
        dvx[window, :] += dot(pb, g, TN)
        return carry

    lax.fori_loop(0, tokens // BLOCK, block_step, 0)
    dk_ref[...] = dkx[WINDOW:]
    dv_ref[...] = dvx[WINDOW:]


def of_head(head, a):
    return pl.BlockSpec((a.shape[0], None) + a.shape[2:], lambda i: (0, head, 0, 0))


def attend(cap, final, counts, first, head, qg, at, prev, own, *sources):
    tokens, head_dim = qg.shape[2:]
    ext = tokens + WINDOW
    slots = 2 * cap + sum(s.shape[0] for s in sources[2:])
    row16 = jax.ShapeDtypeStruct((tokens, head_dim), jnp.bfloat16)
    row32 = jax.ShapeDtypeStruct((tokens, head_dim), jnp.float32)
    return pl.pallas_call(
        functools.partial(attention_kernel, cap),
        out_shape=(row16, row16, jax.ShapeDtypeStruct((2, tokens), jnp.float32), row32, row32),
        grid=(1,),
        in_specs=[SM] * 3 + [of_head(head, qg), of_head(at, prev), of_head(head, own)] + [ANY] * len(sources),
        out_specs=[VM] * 5,
        scratch_shapes=[
            pltpu.VMEM((slots, 2, BLOCK, head_dim), jnp.bfloat16),
            pltpu.VMEM((ext, head_dim), jnp.bfloat16),
            pltpu.VMEM((ext, head_dim), jnp.bfloat16),
            pltpu.VMEM((ext, head_dim), jnp.float32),
            pltpu.VMEM((ext, head_dim), jnp.float32),
            pltpu.SemaphoreType.DMA((len(sources),)),
        ],
        compiler_params=pltpu.CompilerParams(vmem_limit_bytes=32 << 20),
        cost_estimate=pl.CostEstimate(flops=128 * tokens * tokens * head_dim, bytes_accessed=1 << 16, transcendentals=0),
        name="attend",
    )(final, counts, first, qg, prev, own, *sources)


def back_kernel(stat_ref, next_ref, own_ref, dk_in, dv_in, dk_ref, dv_ref):
    tokens, head_dim = dk_in.shape
    scale = 1.0 / math.sqrt(head_dim)
    size = 2 * BLOCK
    for j in range(tokens // size):
        rows = slice(j * size, (j + 1) * size)
        seen = (j + 1) * size
        k, v = own_ref[0, rows], own_ref[1, rows]
        q, g = next_ref[0, :seen], next_ref[1, :seen]
        key = lax.broadcasted_iota(jnp.int32, (size, seen), 0) + j * size
        query = lax.broadcasted_iota(jnp.int32, (size, seen), 1)
        s = dot(k, q, NT) * (scale * LOG2E) - stat_ref[0:1, :seen]
        p = jnp.exp2(jnp.where(key > query, s, MASKED))
        ds = (p * (dot(v, g, NT) - stat_ref[1:2, :seen])).astype(jnp.bfloat16)
        dk_ref[rows] = ((dk_in[rows] + dot(ds, q)) * scale).astype(jnp.bfloat16)
        dv_ref[rows] = (dv_in[rows] + dot(p.astype(jnp.bfloat16), g)).astype(jnp.bfloat16)


def add_back(head, stat, at, following, own, dk, dv):
    tokens, head_dim = dk.shape
    row16 = jax.ShapeDtypeStruct((tokens, head_dim), jnp.bfloat16)
    return pl.pallas_call(
        back_kernel,
        out_shape=(row16, row16),
        grid=(1,),
        in_specs=[VM, of_head(at, following), of_head(head, own), VM, VM],
        out_specs=[VM] * 2,
        compiler_params=pltpu.CompilerParams(vmem_limit_bytes=32 << 20),
        cost_estimate=pl.CostEstimate(flops=0, bytes_accessed=1 << 16, transcendentals=0),
        name="add_back",
    )(stat, following, own, dk, dv)


def after(x, *earlier):
    earlier = [e for e in earlier if e is not None]
    return lax.optimization_barrier((x, *earlier))[0] if earlier else x


def shards(queries, seg_keys, seg_values, mem_keys, mem_values, mem_blocks, mem_count, grad_out):
    tokens, heads, head_dim = queries.shape
    owners = lax.axis_size("seq")
    rank = lax.axis_index("seq")
    n_blocks = tokens // BLOCK
    per = mem_keys.shape[0] // BLOCK
    live_total = n_blocks * (TOPK + 1) // 2
    cap = max(2, 2 * live_total // owners)
    along = [(i, i + 1) for i in range(owners - 1)]
    back = [(i + 1, i) for i in range(owners - 1)]
    shift = lambda d: [(i, (i + d) % owners) for i in range(owners)]

    lists = jnp.concatenate([mem_blocks, mem_count[:, None]], 1)
    lists = lax.all_gather(lists, "head", axis=0, tiled=True).reshape(1, -1)
    while lists.shape[0] < owners:
        size = lists.shape[0]
        with jax.named_scope(f"lists{size}"):
            theirs = lax.ppermute(lists, "seq", [(i, i ^ size) for i in range(owners)])
        lists = jnp.concatenate([lists, theirs], 0)

    first = (rank == 0).astype(jnp.int32)[None]
    major = lambda a: jnp.moveaxis(a, 1, 0)
    kv = jnp.stack([major(seg_keys), major(seg_values)], 0)
    qg = jnp.stack([major(queries), major(grad_out)], 0)

    held_keys, held_values = after((mem_keys, mem_values), lists)
    keys, values = (
        jnp.moveaxis(m.reshape(per, BLOCK, heads, head_dim), 2, 0) for m in (held_keys, held_values)
    )

    def border(cut, *earlier):
        up, down = after((kv[:, cut], qg[:, cut]), *earlier)
        with jax.named_scope(f"prev_kv{cut.start}"):
            up = lax.ppermute(up, "seq", along)
        with jax.named_scope(f"next_qg{cut.start}"):
            down = lax.ppermute(down, "seq", back)
        return up, down

    def in_rows(outs):
        return tuple(jnp.stack([o[i] for o in outs], 1) for i in range(4))

    def finish(head, final, counts, borders, *sources):
        prev_kv, next_qg, at = borders[head]
        o, dq, stat, dk, dv = attend(
            cap, final, counts, first, head, qg, at, prev_kv, kv, *sources
        )
        with jax.named_scope(f"stat{head}"):
            stat = lax.ppermute(stat, "seq", back)
        dk, dv = add_back(head, stat, at, next_qg, kv, dk, dv)
        return o, dq, dk, dv

    def direct():
        packed = lists[jnp.arange(owners) ^ rank].reshape(owners, n_blocks, TOPK + 1)
        ids = packed[:, :, :TOPK].reshape(owners, n_blocks * TOPK)
        counts = packed[:, :, TOPK]
        live = (jnp.arange(TOPK, dtype=jnp.int32) < counts[:, :, None]).reshape(owners, -1)
        owner_of = ids // per
        one_hot = (owner_of[:, :, None] == jnp.arange(owners, dtype=jnp.int32)) & live[:, :, None]
        order = jnp.sum((jnp.cumsum(one_hot.astype(jnp.int32), 1) - 1) * one_hot, 2)
        asked = (owner_of == rank) & live
        chosen = asked[:, :, None] & (order[:, :, None] == jnp.arange(cap, dtype=jnp.int32))
        send_idx = jnp.roll(jnp.sum(jnp.where(chosen, (ids % per)[:, :, None], 0), 1), -rank, 0)
        final = jnp.where(live, ((rank - owner_of) % owners) * cap + order, 0)
        final = lax.dynamic_index_in_dim(final, rank, 0, keepdims=False)
        counts = lax.dynamic_index_in_dim(counts, rank, 0, keepdims=False)
        borders = [border(slice(h, h + 1)) + (0,) for h in range(heads)]
        arrived = []
        for h in range(heads):
            send = jnp.stack([keys[h][send_idx], values[h][send_idx]], 2)
            if h >= 2:
                send = after(send, *arrived[h - 2])
            arrived.append([send[0]] + [lax.ppermute(send[d], "seq", shift(d)) for d in range(1, owners)])
        return in_rows([finish(h, final, counts, borders, *arrived[h]) for h in range(heads)])

    if owners != ROWS * COLUMNS:
        return direct()

    pick_table, pack_table, final, counts, need = route(lists, rank[None], cap, per)
    odd = rank % COLUMNS == 1
    swap = [(i, i ^ 1) for i in range(owners)]
    ups = [(i, i + COLUMNS) for i in range(owners - COLUMNS)]
    downs = [(j, i) for i, j in ups]
    blocks = lambda x: x.reshape(-1, 2, BLOCK, head_dim)
    by_column = lambda a, b: jnp.where(odd, a, b)

    def first_leg(h, *earlier):
        (k, v), (q, g) = after((kv[:, h], qg[:, h]), *earlier)
        return [blocks(x) for x in (by_column(q, k), by_column(g, v), by_column(k, q))], v, g

    tiles, up, down = first_leg(0, lists)
    with jax.named_scope("swap0"):
        tiles = lax.ppermute(jnp.concatenate(tiles, 0), "seq", swap)
    with jax.named_scope("up0"):
        up = lax.ppermute(up, "seq", ups)
    with jax.named_scope("down0"):
        down = lax.ppermute(down, "seq", downs)
    tile = tokens // (2 * BLOCK)
    first_legs = (tiles, up, down)

    def by_rows(length):
        lengths = [2 * cap] + [length] * (ROWS - 2)
        picked = [pick(h, pick_table, keys, values) for h in range(min(2, heads))]
        with jax.named_scope("side0"):
            side = [lax.ppermute(picked[0][1], "seq", swap)]
        legs, borders, lines, outs = [first_legs], [], [], []
        flat = lambda x: x.reshape(tokens, head_dim)

        def complete(h):
            ready = after(counts, lines[h + 1][2]) if h + 1 < heads else counts
            outs.append(finish(h, final, ready, borders, picked[h][0], side[h], *lines[h]))

        earlier = []
        for h in range(heads):
            last = h + 1 == heads
            tiles, up, down = legs[h]
            relay = flat(tiles[2 * tile : 3 * tile])
            crossing = [blocks(by_column(up, down))]
            gate = [outs[h - 2][0]] if h >= 2 else lines[0][2:] if h == 1 else []
            if last:
                rising, sinking = relay, relay
            else:
                next_tiles, rising, sinking = first_leg(h + 1, *gate)
                rising, sinking = by_column(rising, relay), by_column(relay, sinking)
                crossing = [picked[h + 1][1]] + next_tiles + crossing
            sends = [jnp.concatenate(crossing, 0), rising, sinking]
            ordered = pack_table if h else after(pack_table, *sends)
            sends = [list(pack(cap, lengths, ordered, picked[h][0], side[h]))] + sends
            sends = lax.optimization_barrier((sends, earlier))[0]
            sent = []
            for d in range(ROWS - 1):
                with jax.named_scope(f"lines{h}_{d}"):
                    route = [(i, i ^ (COLUMNS * (d + 1))) for i in range(owners)]
                    sent.append(lax.ppermute(sends[0][d], "seq", route))
            lines.append(sent)
            if h == 0:
                ordered = after(pick_table, sent[2])
                picked += [pick(i, ordered, keys, values) for i in range(2, heads)]
            with jax.named_scope(f"swap{h + 1}"):
                swapped = lax.ppermute(sends[1], "seq", swap)
            with jax.named_scope(f"up{h + 1}"):
                risen = lax.ppermute(sends[2], "seq", ups)
            with jax.named_scope(f"down{h + 1}"):
                sunk = lax.ppermute(sends[3], "seq", downs)
            earlier = sent + [swapped, risen, sunk]
            rest = swapped
            if not last:
                side.append(swapped)
                legs.append((swapped[ROWS * cap : ROWS * cap + 3 * tile], risen, sunk))
                rest = swapped[ROWS * cap + 3 * tile :]
            near = jnp.stack([flat(tiles[:tile]), flat(tiles[tile : 2 * tile])])
            before = by_column(near, jnp.stack([risen, flat(rest)]))
            behind = by_column(jnp.stack([sunk, flat(rest)]), near)
            borders.append((before[:, None], behind[:, None], 0))
            if h >= 1:
                complete(h - 1)
                earlier.append(outs[h - 1][0])
            if h >= 2:
                earlier.append(outs[h - 2][2])
        complete(heads - 1)
        return in_rows(outs)

    longest = 2 * cap
    sizes = [longest - 2, longest - 1, longest]
    index = jnp.clip(need[0] - sizes[0], 0, 2)
    return lax.switch(index, [functools.partial(by_rows, n) for n in sizes])


def solution(mesh):
    rows = P("seq", "head", None)
    return jax.shard_map(
        shards,
        mesh=mesh,
        in_specs=(rows, rows, rows, rows, rows, P(("seq", "head"), None), P(("seq", "head")), rows),
        out_specs=(rows, rows, rows, rows),
        check_vma=False,
    )
```
